32 devices in a mesh: dp: 8 (over y, x, core), mp: 4 (over z).
Axes of the slice: x: 2, y: 2, z: 4, core: 2. Of those that a mesh axis runs over, the one named last changes fastest.
Arguments:
- token_factors: bfloat16 [4, 16384, 128], P('mp', 'dp'), may hold values from -6 to 6
- example_ids: int32 [8, 2048], P('dp'), may hold values from 0 to 7, never falling along the last dimension, each value on 1 to 1024 neighbouring positions
- left_factor: bfloat16 [4, 64, 64], P('mp'), may hold values from -0.75 to 0.75
- right_factor: bfloat16 [4, 64, 64], P('mp'), may hold values from -0.75 to 0.75
- query_features: bfloat16 [768, 16384], P('dp', 'mp'), may hold values from -0.375 to 0.375
Outputs:
- influence: float32 [768, 64], P(('dp', 'mp'))
The draws below stay inside these ranges and needn't reach their ends.
Inputs may be any that keep to these rules, and one draw needn't show every extreme that they name: `example_ids`: each row is non-decreasing, and every example 0 to 7 has 1 to 1024 tokens in each block.
All inputs are finite; a program needn't handle non-finite values.
Results may differ from the reference program's by a relative error of at most 0.0029.
Values may be sent and summed in bfloat16 or wider, within the bound.
A program may use at most 64 MiB of HBM per device.

```python
import math
import jax
import jax.numpy as jnp
import numpy as np
from jax import lax

R = 64
TOK_DEV = 2048
EX_DEV = 8
LAYERS = 4
BLOCKS = 8
TOKENS = 16384
TRAIN = 64
QUERIES = 768
FEAT = 16384


def levels(stream_key, dims, pieces, smallest, high):
    factor_of = 1.0
    for dim, parts in pieces:
        draws = jax.random.uniform(jax.random.fold_in(jax.random.fold_in(stream_key, 6), dim), (parts,), jnp.float32, smallest / len(pieces), high / len(pieces))
        factor_of = factor_of * jnp.repeat(jnp.exp(draws), dims[dim] // parts).reshape((-1,) + (1,) * (len(dims) - 1 - dim))
    return factor_of


def profile(amount, total, reach, skew):
    portions = [(1 << 20) // math.isqrt(grade ** skew) + 1 for grade in range(2, amount + 1)]
    surplus, given = total - reach - (amount - 1), [1] * (amount - 1)
    while surplus > 0:
        movable = [i for i in range(amount - 1) if given[i] < reach]
        whole, remaining = sum([portions[i] for i in movable]), surplus
        for i in movable:
            more = min(reach - given[i], max(1, remaining * portions[i] // whole), surplus)
            given[i] = given[i] + more
            surplus = surplus - more
    return np.array([reach] + given)


def ragged_sizes(own_key, amount, total, bound, lean):
    if amount == 2:
        one = jax.random.randint(own_key, (), max(1, total - bound), min(bound, total - 1) + 1)
        return jnp.stack([one, total - one])
    tallies = jnp.asarray(profile(amount, total, bound, lean), jnp.int32)
    pairs = (amount - 1) // 2
    giver, sink = tallies[1:1 + 2 * pairs:2], tallies[2:2 + 2 * pairs:2]
    margin = jnp.minimum(giver - 1, bound - sink)
    moved = jax.random.randint(jax.random.fold_in(own_key, 1), (pairs,), 0, 1 << 20) % (margin + 1)
    tallies = tallies.at[1:1 + 2 * pairs:2].set(giver - moved).at[2:2 + 2 * pairs:2].set(sink + moved)
    return tallies[jax.random.permutation(jax.random.fold_in(own_key, 2), amount)]


def noise(key, shape, width, reach, cuts=(), kind=jnp.bfloat16):
    array = width * jax.random.normal(key, shape, jnp.float32)
    if cuts:
        array = array * levels(key, shape, cuts, -0.22, 0.18)
    return jnp.clip(array, -reach, reach).astype(kind)


def setup_inputs(seed: int = 0) -> dict:
    keys = jax.random.split(jax.random.key(seed), 6)
    return {
        "token_factors": noise(keys[0], (LAYERS, TOKENS, 2 * R), 1.0, 6.0, ((0, 4), (1, 8))),
        "example_ids": jax.vmap(lambda own: jnp.searchsorted(jnp.cumsum(ragged_sizes(own, EX_DEV, TOK_DEV, TOK_DEV // 2, 0)), jnp.arange(TOK_DEV), side="right"))(jax.random.split(keys[1], BLOCKS)).reshape((BLOCKS, TOK_DEV)).astype(jnp.int32),
        "left_factor": noise(keys[2], (LAYERS, R, R), R ** -0.5, 0.75, ((0, 4),)),
        "right_factor": noise(keys[3], (LAYERS, R, R), R ** -0.5, 0.75, ((0, 4),)),
        "query_features": noise(keys[4], (QUERIES, FEAT), (LAYERS * R) ** -0.5, 0.375, ((0, 8), (1, 4))),
    }


def precondition(factors, labels, left, right):
    inputs = factors[:, :R].astype(jnp.float32)
    outputs = factors[:, R:].astype(jnp.float32)
    outer = outputs[:, :, None] * inputs[:, None, :]
    summed = jax.ops.segment_sum(outer, labels, num_segments=EX_DEV)
    counts = jax.ops.segment_sum(jnp.ones(labels.shape, jnp.float32), labels, num_segments=EX_DEV)
    gradient = summed / counts[:, None, None]
    precond = jnp.einsum("ac,ecd,db->eab", left.astype(jnp.float32), gradient, right.astype(jnp.float32), precision=lax.Precision.HIGHEST)
    return precond.reshape(EX_DEV, R * R)


def reference(token_factors, example_ids, left_factor, right_factor, query_features):
    def one_block(index):
        factors = lax.dynamic_slice_in_dim(token_factors, index * TOK_DEV, TOK_DEV, axis=1)
        labels = example_ids[index]

        def one_layer(item):
            return precondition(item[0], labels, item[1], item[2])

        per_layer = lax.map(one_layer, (factors, left_factor, right_factor))
        return jnp.transpose(per_layer, (1, 0, 2)).reshape(EX_DEV, LAYERS * R * R)

    features = lax.map(one_block, jnp.arange(BLOCKS, dtype=jnp.int32))
    features = features.reshape(TRAIN, LAYERS * R * R).astype(jnp.bfloat16)
    queries = query_features.reshape(QUERIES, LAYERS, R * R)
    trains = features.reshape(TRAIN, LAYERS, R * R)

    def add_layer(total, layer):
        query_part = lax.dynamic_index_in_dim(queries, layer, axis=1, keepdims=False)
        train_part = lax.dynamic_index_in_dim(trains, layer, axis=1, keepdims=False)
        return total + jnp.dot(query_part, train_part.T, preferred_element_type=jnp.float32), None

    total, unused = lax.scan(add_layer, jnp.zeros((QUERIES, TRAIN), jnp.float32), jnp.arange(LAYERS, dtype=jnp.int32))
    return total
```

```python
import functools

import jax
import jax.numpy as jnp
from jax import lax
from jax.experimental import pallas as pl
from jax.experimental.pallas import tpu as pltpu
from jax.sharding import PartitionSpec as P

EX_DEV = 8
LANES = 128
F32, BF16 = jnp.float32, jnp.bfloat16
NT = (((1,), (1,)), ((), ()))


def flipped(index, mask):
    bit = 1
    while bit <= mask:
        if mask & bit:
            index = index + bit - 2 * bit * ((index // bit) % 2)
        bit *= 2
    return index


def partner(index, offset, count):
    if count & (count - 1) == 0:
        return flipped(index, offset)
    return (index + offset) % count


def iota(shape, dim):
    return lax.broadcasted_iota(jnp.int32, shape, dim)


def split(value):
    high = value.astype(BF16)
    return high, (value - high.astype(F32)).astype(BF16)


def kernel(
    n_dp, n_mp,
    tokens_hbm, ids_ref, left_ref, right_ref, query_hbm, out_ref,
    tok, qbuf, masked, fsend, fall, part, prec,
    tok_sem, q_sem, qx_send, qx_recv, f_send, f_recv, p_send, p_recv,
):
    d, m = lax.axis_index("dp"), lax.axis_index("mp")
    core = d % 2
    sibling = flipped(d, 1)
    tokens = tok.shape[0]
    rank = left_ref.shape[1]
    rows_q = query_hbm.shape[0]
    half = query_hbm.shape[1] // 2
    quarter = half // 2
    rows_out = rows_q // n_mp
    groups = 2 * n_mp

    load_tokens = pltpu.make_async_copy(tokens_hbm.at[0], tok, tok_sem)
    load_tokens.start()

    barrier = pltpu.get_barrier_semaphore()
    for k in range(1, n_dp):
        pl.semaphore_signal(barrier, inc=1, device_id={"dp": partner(d, k, n_dp), "mp": m})
    for k in range(1, n_mp):
        for s in range(2):
            pl.semaphore_signal(
                barrier, inc=1, device_id={"dp": flipped(d, s), "mp": partner(m, k, n_mp)}
            )

    def half_of(which):
        return pl.ds(pl.multiple_of(which * half, LANES), half)

    my_rows = pl.ds(pl.multiple_of(core * rows_q, 16), rows_q)
    load_query = pltpu.make_async_copy(query_hbm.at[:, half_of(core)], qbuf.at[my_rows], q_sem)
    load_query.start()

    ids = ids_ref[...]
    member = (ids == iota((EX_DEV, tokens), 0)).astype(F32)
    counts = jnp.sum(member, axis=1, keepdims=True)

    pick = (iota((rank, 2 * rank), 1) == iota((rank, 2 * rank), 0) + rank).astype(BF16)
    spread = (iota((rank, rank * EX_DEV), 1) // EX_DEV == iota((rank, rank * EX_DEV), 0)).astype(BF16)
    same = (iota((EX_DEV, rank * EX_DEV), 1) % EX_DEV == iota((EX_DEV, rank * EX_DEV), 0)).astype(F32)
    left_wide = jnp.dot(left_ref[0], spread, preferred_element_type=F32)
    left_kron = (left_wide[:, None, :] * same[None]).reshape(rank * EX_DEV, rank * EX_DEV).astype(BF16)
    right = right_ref[0]
    right_row = jnp.concatenate([right, right], axis=1)
    right_all = jnp.concatenate([right_row, right_row], axis=0)

    load_tokens.wait()
    step = 256
    for start in range(0, tokens, step):
        outputs = lax.dot_general(pick, tok[start:start + step, :], NT, preferred_element_type=F32)
        chosen = outputs[:, None, :] * member[None, :, start:start + step]
        masked[:, start:start + step] = chosen.reshape(rank * EX_DEV, step).astype(BF16)
    summed = jnp.dot(masked[...], tok[...], preferred_element_type=F32)
    grad = (summed.reshape(rank, EX_DEV, 2 * rank) / counts[None]).reshape(rank * EX_DEV, 2 * rank)
    lower = iota((rank * EX_DEV, 2 * rank), 1) < rank
    high, low = split(grad)
    low_moved = pltpu.roll(grad - high.astype(F32), rank, 1)
    both = jnp.where(lower, grad, low_moved).astype(BF16)
    high, low = split(jnp.dot(left_kron, both, preferred_element_type=F32))
    precond = jnp.dot(high, right_all, preferred_element_type=F32) + jnp.dot(
        low, right_all, preferred_element_type=F32
    )
    paired = precond.reshape(rank // 2, 2, EX_DEV, 2 * rank)
    lower_small = iota((EX_DEV, 2 * rank), 1) < rank
    pairs_quarter = rank // 8
    for h in range(2):
        for j in range(pairs_quarter):
            two = []
            for q in range(2):
                at = (h * 2 + q) * pairs_quarter + j
                two.append(jnp.where(lower_small, paired[at, 0], paired[at, 1]))
            fsend[h, :, j * LANES:(j + 1) * LANES] = jnp.concatenate(two, axis=0).astype(BF16)

    pl.semaphore_wait(barrier, n_dp - 1 + 2 * (n_mp - 1))

    copies = []
    for k in range(n_dp - 1, 0, -1):
        to = partner(d, k, n_dp)
        copy = pltpu.make_async_remote_copy(
            src_ref=fsend.at[to % 2],
            dst_ref=fall.at[d],
            send_sem=f_send.at[to],
            recv_sem=f_recv.at[d],
            device_id={"dp": to, "mp": m},
            device_id_type=pl.DeviceIdType.MESH,
        )
        copy.start()
        copies.append((to, copy))
    query_copy = pltpu.make_async_remote_copy(
        src_ref=query_hbm.at[:, half_of(1 - core)],
        dst_ref=qbuf.at[my_rows],
        send_sem=qx_send,
        recv_sem=qx_recv,
        device_id={"dp": sibling, "mp": m},
        device_id_type=pl.DeviceIdType.MESH,
    )
    query_copy.start()
    fall[d] = fsend[core]

    load_query.wait()
    their_rows = pl.ds(pl.multiple_of((1 - core) * rows_q, 16), rows_q)
    pltpu.make_async_remote_copy(
        src_ref=query_hbm.at[:, half_of(1 - core)],
        dst_ref=qbuf.at[their_rows],
        send_sem=qx_send,
        recv_sem=qx_recv,
        device_id={"dp": sibling, "mp": m},
        device_id_type=pl.DeviceIdType.MESH,
    ).wait_recv()
    for k in range(1, n_dp):
        source = partner(d, k, n_dp) if n_dp & (n_dp - 1) == 0 else (d + n_dp - k) % n_dp
        pltpu.make_async_remote_copy(
            src_ref=fsend.at[0],
            dst_ref=fall.at[source],
            send_sem=f_send.at[source],
            recv_sem=f_recv.at[source],
            device_id={"dp": source, "mp": m},
            device_id_type=pl.DeviceIdType.MESH,
        ).wait_recv()

    feats = fall[...].reshape(n_dp * 2 * EX_DEV, quarter)
    score = []
    for q in range(2):
        score.append(
            lax.dot_general(
                feats, qbuf[:, q * quarter:(q + 1) * quarter], NT, preferred_element_type=F32
            ).reshape(n_dp, 2, EX_DEV, 2 * rows_q)[:, q]
        )
    scores = (score[0] + score[1]).reshape(n_dp * EX_DEV, 2 * rows_q).T
    part[...] = scores.reshape(groups, rows_out, n_dp * EX_DEV)

    mine = core * n_mp + m
    sent = []
    for k in range(n_mp):
        for s in range(2):
            if k == 0 and s == 0:
                continue
            to_m = partner(m, k, n_mp)
            to_core = flipped(core, s)
            slot = to_core * n_mp + to_m
            copy = pltpu.make_async_remote_copy(
                src_ref=part.at[slot],
                dst_ref=prec.at[mine],
                send_sem=p_send.at[slot],
                recv_sem=p_recv.at[mine],
                device_id={"dp": flipped(d, s), "mp": to_m},
                device_id_type=pl.DeviceIdType.MESH,
            )
            copy.start()
            sent.append(copy)
    total = part[mine]
    for k in range(n_mp):
        for s in range(2):
            if k == 0 and s == 0:
                continue
            from_m = partner(m, k, n_mp) if n_mp & (n_mp - 1) == 0 else (m + n_mp - k) % n_mp
            slot = flipped(core, s) * n_mp + from_m
            pltpu.make_async_remote_copy(
                src_ref=part.at[slot],
                dst_ref=prec.at[slot],
                send_sem=p_send.at[slot],
                recv_sem=p_recv.at[slot],
                device_id={"dp": flipped(d, s), "mp": from_m},
                device_id_type=pl.DeviceIdType.MESH,
            ).wait_recv()
            total = total + prec[slot]
    out_ref[...] = total
    for to, copy in copies:
        copy.wait_send()
    query_copy.wait_send()
    for copy in sent:
        copy.wait_send()


def shards(n_dp, n_mp, token_factors, example_ids, left_factor, right_factor, query_features):
    tokens, rank = token_factors.shape[1], left_factor.shape[1]
    rows_q, feat = query_features.shape
    rows_out = rows_q // n_mp
    groups = 2 * n_mp
    train = n_dp * EX_DEV
    dma = pltpu.SemaphoreType.DMA
    vmem = pl.BlockSpec(memory_space=pltpu.VMEM)
    anywhere = pl.BlockSpec(memory_space=pl.ANY)
    return pl.pallas_call(
        functools.partial(kernel, n_dp, n_mp),
        out_shape=jax.ShapeDtypeStruct((rows_out, train), F32),
        in_specs=[anywhere, vmem, vmem, vmem, anywhere],
        out_specs=vmem,
        scratch_shapes=[
            pltpu.VMEM((tokens, 2 * rank), BF16),
            pltpu.VMEM((2 * rows_q, feat // 2), BF16),
            pltpu.VMEM((rank * EX_DEV, tokens), BF16),
            pltpu.VMEM((2, 2 * EX_DEV, feat // 4), BF16),
            pltpu.VMEM((n_dp, 2 * EX_DEV, feat // 4), BF16),
            pltpu.VMEM((groups, rows_out, train), F32),
            pltpu.VMEM((groups, rows_out, train), F32),
            dma, dma, dma, dma,
            dma((n_dp,)), dma((n_dp,)),
            dma((groups,)), dma((groups,)),
        ],
        compiler_params=pltpu.CompilerParams(
            collective_id=0, has_side_effects=True, vmem_limit_bytes=40 * 1024 * 1024
        ),
        cost_estimate=pl.CostEstimate(
            flops=2 * rank * EX_DEV * tokens * 2 * rank, bytes_accessed=2 * rows_q * feat,
            transcendentals=0,
        ),
    )(token_factors, example_ids, left_factor, right_factor, query_features)


def solution(mesh):
    placed = (
        P("mp", "dp", None),
        P("dp", None),
        P("mp", None, None),
        P("mp", None, None),
        P("dp", "mp"),
    )
    return jax.shard_map(
        functools.partial(shards, mesh.shape["dp"], mesh.shape["mp"]),
        mesh=mesh, in_specs=placed, out_specs=P(("dp", "mp"), None), check_vma=False,
    )
```

```python
import functools

import jax
import jax.numpy as jnp
from jax import lax
from jax.experimental import pallas as pl
from jax.experimental.pallas import tpu as pltpu
from jax.sharding import PartitionSpec as P

EX_DEV = 8
LANES = 128
F32, BF16 = jnp.float32, jnp.bfloat16
NT = (((1,), (1,)), ((), ()))


def flipped(index, mask):
    bit = 1
    while bit <= mask:
        if mask & bit:
            index = index + bit - 2 * bit * ((index // bit) % 2)
        bit *= 2
    return index


def partner(index, offset, count):
    if count & (count - 1) == 0:
        return flipped(index, offset)
    return (index + offset) % count


def iota(shape, dim):
    return lax.broadcasted_iota(jnp.int32, shape, dim)


def split(value):
    high = value.astype(BF16)
    return high, (value - high.astype(F32)).astype(BF16)


def kernel(
    n_dp, n_mp,
    tokens_hbm, ids_hbm, left_hbm, right_hbm, query_hbm, out_ref,
    tok, ids_ref, left_ref, right_ref, blocks, pscr, qbuf, fsend, fall, part, prec,
    in_sem, q_sem, qx_send, qx_recv, f_send, f_recv, p_send, p_recv,
):
    d, m = lax.axis_index("dp"), lax.axis_index("mp")
    core = d % 2
    sibling = flipped(d, 1)
    tokens = tok.shape[0]
    rank = left_ref.shape[0]
    rows_q = query_hbm.shape[0]
    half = query_hbm.shape[1] // 2
    quarter = half // 2
    rows_out = rows_q // n_mp
    groups = 2 * n_mp

    loads = []
    for i, (source, target) in enumerate(
        ((tokens_hbm.at[0], tok), (ids_hbm, ids_ref), (left_hbm.at[0], left_ref), (right_hbm.at[0], right_ref))
    ):
        loads.append(pltpu.make_async_copy(source, target, in_sem.at[i]))
        loads[-1].start()

    barrier = pltpu.get_barrier_semaphore()
    for k in range(1, n_dp):
        pl.semaphore_signal(barrier, inc=1, device_id={"dp": partner(d, k, n_dp), "mp": m})
    for k in range(1, n_mp):
        for s in range(2):
            pl.semaphore_signal(
                barrier, inc=1, device_id={"dp": flipped(d, s), "mp": partner(m, k, n_mp)}
            )

    def half_of(which):
        return pl.ds(pl.multiple_of(which * half, LANES), half)

    my_rows = pl.ds(pl.multiple_of(core * rows_q, 16), rows_q)
    load_query = pltpu.make_async_copy(query_hbm.at[:, half_of(core)], qbuf.at[my_rows], q_sem)
    load_query.start()

    loads[1].wait()
    ids = ids_ref[...]
    one, zero = jnp.ones((rank, tokens), BF16), jnp.zeros((rank, tokens), BF16)
    by_low = jnp.concatenate([jnp.where(ids % 2 == i, one, zero) for i in range(2)], axis=0)
    by_high = jnp.concatenate([jnp.where(ids // 2 == j, one, zero) for j in range(4)], axis=0)
    counts = lax.dot_general(by_low, by_high, NT, preferred_element_type=F32)

    loads[2].wait()
    loads[3].wait()
    tall = 2 * rank
    widen = (iota((rank, tall), 1) % rank == iota((rank, tall), 0)).astype(BF16)
    rows = (
        iota((tall, rank), 1) == 2 * (iota((tall, rank), 0) % (rank // 2)) + iota((tall, rank), 0) // rank
    ).astype(BF16)
    left = jnp.dot(left_ref[...], widen, preferred_element_type=F32).astype(BF16)
    left = jnp.dot(rows, left, preferred_element_type=F32)
    same = iota((tall, tall), 1) // rank == (iota((tall, tall), 0) // (rank // 2)) % 2
    left = jnp.where(same, left, 0.0).astype(BF16)
    left = jnp.concatenate([left, left], axis=1)
    wide = EX_DEV * rank
    widest = (iota((rank, wide), 1) % rank == iota((rank, wide), 0)).astype(BF16)
    right = jnp.dot(right_ref[...], widest, preferred_element_type=F32)
    column = iota((rank, wide), 1) // rank
    for p in range(2):
        for j in range(4):
            at = (p * 4 + j) * rank
            blocks[at:at + rank, :] = jnp.where(column == 2 * j + p, right, 0.0).astype(BF16)

    turn = (iota((tall, tall), 1) == iota((tall, tall), 0)).astype(BF16)
    loads[0].wait()
    turned = lax.dot_general(turn, tok[...], NT, preferred_element_type=F32).astype(BF16)
    inputs, outputs = turned[:rank], turned[rank:]
    lhs = jnp.concatenate([outputs] * 2, axis=0) * by_low
    rhs = jnp.concatenate([inputs] * 4, axis=0) * by_high
    grad = lax.dot_general(lhs, rhs, NT, preferred_element_type=F32) / counts
    high, low = split(grad)
    mixed = jnp.dot(left, jnp.concatenate([high, low], axis=0), preferred_element_type=F32)
    high, low = split(jnp.concatenate([mixed[:rank], mixed[rank:]], axis=1))
    both = jnp.dot(jnp.concatenate([high, low], axis=0), blocks[...], preferred_element_type=F32)
    precond = both[:rank] + both[rank:]
    for j in range(4):
        pscr[j * rank:(j + 1) * rank, :] = precond[:, j * LANES:(j + 1) * LANES]
    spread = rank // 2
    tiles = spread // 4
    for h in range(2):
        for j in range(tiles):
            two = [
                pscr[pl.ds((h * 2 + q) * tiles + j, EX_DEV, stride=spread), :] for q in range(2)
            ]
            fsend[h, :, j * LANES:(j + 1) * LANES] = jnp.concatenate(two, axis=0).astype(BF16)

    pl.semaphore_wait(barrier, n_dp - 1 + 2 * (n_mp - 1))

    copies = []
    for k in range(n_dp - 1, 0, -1):
        to = partner(d, k, n_dp)
        copy = pltpu.make_async_remote_copy(
            src_ref=fsend.at[to % 2],
            dst_ref=fall.at[d],
            send_sem=f_send.at[to],
            recv_sem=f_recv.at[d],
            device_id={"dp": to, "mp": m},
            device_id_type=pl.DeviceIdType.MESH,
        )
        copy.start()
        copies.append((to, copy))
    query_copy = pltpu.make_async_remote_copy(
        src_ref=query_hbm.at[:, half_of(1 - core)],
        dst_ref=qbuf.at[my_rows],
        send_sem=qx_send,
        recv_sem=qx_recv,
        device_id={"dp": sibling, "mp": m},
        device_id_type=pl.DeviceIdType.MESH,
    )
    query_copy.start()
    fall[d] = fsend[core]

    load_query.wait()
    their_rows = pl.ds(pl.multiple_of((1 - core) * rows_q, 16), rows_q)
    pltpu.make_async_remote_copy(
        src_ref=query_hbm.at[:, half_of(1 - core)],
        dst_ref=qbuf.at[their_rows],
        send_sem=qx_send,
        recv_sem=qx_recv,
        device_id={"dp": sibling, "mp": m},
        device_id_type=pl.DeviceIdType.MESH,
    ).wait_recv()
    for k in range(1, n_dp):
        source = partner(d, k, n_dp) if n_dp & (n_dp - 1) == 0 else (d + n_dp - k) % n_dp
        pltpu.make_async_remote_copy(
            src_ref=fsend.at[0],
            dst_ref=fall.at[source],
            send_sem=f_send.at[source],
            recv_sem=f_recv.at[source],
            device_id={"dp": source, "mp": m},
            device_id_type=pl.DeviceIdType.MESH,
        ).wait_recv()

    feats = fall[...].reshape(n_dp * 2 * EX_DEV, quarter)
    score = []
    for q in range(2):
        score.append(
            lax.dot_general(
                feats, qbuf[:, q * quarter:(q + 1) * quarter], NT, preferred_element_type=F32
            ).reshape(n_dp, 2, EX_DEV, 2 * rows_q)[:, q]
        )
    scores = (score[0] + score[1]).reshape(n_dp * EX_DEV, 2 * rows_q).T
    part[...] = scores.reshape(groups, rows_out, n_dp * EX_DEV)

    mine = core * n_mp + m
    sent = []
    for k in range(n_mp):
        for s in range(2):
            if k == 0 and s == 0:
                continue
            to_m = partner(m, k, n_mp)
            to_core = flipped(core, s)
            slot = to_core * n_mp + to_m
            copy = pltpu.make_async_remote_copy(
                src_ref=part.at[slot],
                dst_ref=prec.at[mine],
                send_sem=p_send.at[slot],
                recv_sem=p_recv.at[mine],
                device_id={"dp": flipped(d, s), "mp": to_m},
                device_id_type=pl.DeviceIdType.MESH,
            )
            copy.start()
            sent.append(copy)
    total = part[mine]
    for k in range(n_mp):
        for s in range(2):
            if k == 0 and s == 0:
                continue
            from_m = partner(m, k, n_mp) if n_mp & (n_mp - 1) == 0 else (m + n_mp - k) % n_mp
            slot = flipped(core, s) * n_mp + from_m
            pltpu.make_async_remote_copy(
                src_ref=part.at[slot],
                dst_ref=prec.at[slot],
                send_sem=p_send.at[slot],
                recv_sem=p_recv.at[slot],
                device_id={"dp": flipped(d, s), "mp": from_m},
                device_id_type=pl.DeviceIdType.MESH,
            ).wait_recv()
            total = total + prec[slot]
    out_ref[...] = total
    for to, copy in copies:
        copy.wait_send()
    query_copy.wait_send()
    for copy in sent:
        copy.wait_send()


def shards(n_dp, n_mp, token_factors, example_ids, left_factor, right_factor, query_features):
    tokens, rank = token_factors.shape[1], left_factor.shape[1]
    rows_q, feat = query_features.shape
    rows_out = rows_q // n_mp
    groups = 2 * n_mp
    train = n_dp * EX_DEV
    dma = pltpu.SemaphoreType.DMA
    vmem = pl.BlockSpec(memory_space=pltpu.VMEM)
    in_hbm = pl.BlockSpec(memory_space=pltpu.HBM)
    return pl.pallas_call(
        functools.partial(kernel, n_dp, n_mp),
        out_shape=jax.ShapeDtypeStruct((rows_out, train), F32),
        in_specs=[in_hbm] * 5,
        out_specs=vmem,
        scratch_shapes=[
            pltpu.VMEM((tokens, 2 * rank), BF16),
            pltpu.VMEM((1, tokens), jnp.int32),
            pltpu.VMEM((rank, rank), BF16),
            pltpu.VMEM((rank, rank), BF16),
            pltpu.VMEM((EX_DEV * rank, EX_DEV * rank), BF16),
            pltpu.VMEM((4 * rank, 2 * rank), F32),
            pltpu.VMEM((2 * rows_q, feat // 2), BF16),
            pltpu.VMEM((2, 2 * EX_DEV, feat // 4), BF16),
            pltpu.VMEM((n_dp, 2 * EX_DEV, feat // 4), BF16),
            pltpu.VMEM((groups, rows_out, train), F32),
            pltpu.VMEM((groups, rows_out, train), F32),
            dma((4,)), dma, dma, dma,
            dma((n_dp,)), dma((n_dp,)),
            dma((groups,)), dma((groups,)),
        ],
        compiler_params=pltpu.CompilerParams(
            collective_id=0, has_side_effects=True, vmem_limit_bytes=56 * 1024 * 1024
        ),
        cost_estimate=pl.CostEstimate(
            flops=2 * rank * EX_DEV * tokens * 2 * rank, bytes_accessed=2 * rows_q * feat,
            transcendentals=0,
        ),
    )(token_factors, example_ids, left_factor, right_factor, query_features)


def solution(mesh):
    placed = (
        P("mp", "dp", None),
        P("dp", None),
        P("mp", None, None),
        P("mp", None, None),
        P("dp", "mp"),
    )
    return jax.shard_map(
        functools.partial(shards, mesh.shape["dp"], mesh.shape["mp"]),
        mesh=mesh, in_specs=placed, out_specs=P(("dp", "mp"), None), check_vma=False,
    )
```

```python
import functools

import jax
import jax.numpy as jnp
from jax import lax
from jax.experimental import pallas as pl
from jax.experimental.pallas import tpu as pltpu
from jax.sharding import PartitionSpec as P

EX_DEV = 8
LANES = 128
F32, BF16 = jnp.float32, jnp.bfloat16
NT = (((1,), (1,)), ((), ()))


def flipped(index, mask):
    bit = 1
    while bit <= mask:
        if mask & bit:
            index = index + bit - 2 * bit * ((index // bit) % 2)
        bit *= 2
    return index


def partner(index, offset, count):
    if count & (count - 1) == 0:
        return flipped(index, offset)
    return (index + offset) % count


def iota(shape, dim):
    return lax.broadcasted_iota(jnp.int32, shape, dim)


def split(value):
    high = value.astype(BF16)
    return high, (value - high.astype(F32)).astype(BF16)


def kernel(
    n_dp, n_mp,
    tokens_hbm, ids_hbm, left_hbm, right_hbm, query_hbm, out_ref,
    tok, ids_ref, left_ref, right_ref, blocks, pscr, qbuf, fsend, fall, part, prec,
    in_sem, q_sem, qx_send, qx_recv, f_send, f_recv, p_send, p_recv,
):
    d, m = lax.axis_index("dp"), lax.axis_index("mp")
    core = d % 2
    sibling = flipped(d, 1)
    tokens = tok.shape[0]
    rank = left_ref.shape[0]
    rows_q = query_hbm.shape[0]
    half = query_hbm.shape[1] // 2
    quarter = half // 2
    rows_out = rows_q // n_mp
    groups = 2 * n_mp

    loads = []
    for i, (source, target) in enumerate(
        ((tokens_hbm.at[0], tok), (ids_hbm, ids_ref), (left_hbm.at[0], left_ref), (right_hbm.at[0], right_ref))
    ):
        loads.append(pltpu.make_async_copy(source, target, in_sem.at[i]))
        loads[-1].start()

    barrier = pltpu.get_barrier_semaphore()
    for k in range(1, n_dp):
        pl.semaphore_signal(barrier, inc=1, device_id={"dp": partner(d, k, n_dp), "mp": m})
    for k in range(1, n_mp):
        for s in range(2):
            pl.semaphore_signal(
                barrier, inc=1, device_id={"dp": flipped(d, s), "mp": partner(m, k, n_mp)}
            )

    def half_of(which):
        return pl.ds(pl.multiple_of(which * half, LANES), half)

    my_rows = pl.ds(pl.multiple_of(core * rows_q, 16), rows_q)
    load_query = pltpu.make_async_copy(query_hbm.at[:, half_of(core)], qbuf.at[my_rows], q_sem)
    load_query.start()

    for load in loads:
        load.wait()
    pl.semaphore_wait(barrier, n_dp - 1 + 2 * (n_mp - 1))

    query_copy = pltpu.make_async_remote_copy(
        src_ref=query_hbm.at[:, half_of(1 - core)],
        dst_ref=qbuf.at[my_rows],
        send_sem=qx_send,
        recv_sem=qx_recv,
        device_id={"dp": sibling, "mp": m},
        device_id_type=pl.DeviceIdType.MESH,
    )
    query_copy.start()

    tall, wide = 2 * rank, EX_DEV * rank
    ids = ids_ref[...]
    member = (ids == iota((EX_DEV, tokens), 0)).astype(F32)
    inverse = 1.0 / jnp.sum(member, axis=1, keepdims=True)
    group = iota((1, 4 * rank), 1) // rank
    scale = []
    for i in range(2):
        row = jnp.zeros((1, 4 * rank), F32)
        for j in range(4):
            row = jnp.where(group == j, inverse[2 * j + i:2 * j + i + 1, :], row)
        scale.append(jnp.broadcast_to(row, (rank, 4 * rank)))
    scale = jnp.concatenate(scale, axis=0)

    step = 512
    turn = (iota((tall, tall), 1) == iota((tall, tall), 0)).astype(BF16)
    none = jnp.zeros((rank, step), BF16)
    summed = jnp.zeros((tall, 4 * rank), F32)
    for start in range(0, tokens, step):
        turned = lax.dot_general(
            turn, tok[start:start + step, :], NT, preferred_element_type=F32
        ).astype(BF16)
        inputs, outputs = turned[:rank], turned[rank:]
        here = ids[:, start:start + step]
        lhs = jnp.concatenate([jnp.where(here % 2 == i, outputs, none) for i in range(2)], axis=0)
        rhs = jnp.concatenate([jnp.where(here // 2 == j, inputs, none) for j in range(4)], axis=0)
        summed = summed + lax.dot_general(lhs, rhs, NT, preferred_element_type=F32)
    grad = summed * scale

    widen = (iota((rank, tall), 1) % rank == iota((rank, tall), 0)).astype(BF16)
    rows = (
        iota((tall, rank), 1) == 2 * (iota((tall, rank), 0) % (rank // 2)) + iota((tall, rank), 0) // rank
    ).astype(BF16)
    left = jnp.dot(left_ref[...], widen, preferred_element_type=F32).astype(BF16)
    left = jnp.dot(rows, left, preferred_element_type=F32)
    same = iota((tall, tall), 1) // rank == (iota((tall, tall), 0) // (rank // 2)) % 2
    left = jnp.where(same, left, 0.0).astype(BF16)
    left = jnp.concatenate([left, left], axis=1)
    widest = (iota((rank, wide), 1) % rank == iota((rank, wide), 0)).astype(BF16)
    right = jnp.dot(right_ref[...], widest, preferred_element_type=F32)
    column = iota((rank, wide), 1) // rank
    for p in range(2):
        for j in range(4):
            at = (p * 4 + j) * rank
            blocks[at:at + rank, :] = jnp.where(column == 2 * j + p, right, 0.0).astype(BF16)

    high, low = split(grad)
    mixed = jnp.dot(left, jnp.concatenate([high, low], axis=0), preferred_element_type=F32)
    high, low = split(jnp.concatenate([mixed[:rank], mixed[rank:]], axis=1))
    both = jnp.dot(jnp.concatenate([high, low], axis=0), blocks[...], preferred_element_type=F32)
    precond = both[:rank] + both[rank:]
    for j in range(4):
        pscr[j * rank:(j + 1) * rank, :] = precond[:, j * LANES:(j + 1) * LANES]
    spread = rank // 2
    tiles = spread // 4
    for h in range(2):
        for j in range(tiles):
            two = [
                pscr[pl.ds((h * 2 + q) * tiles + j, EX_DEV, stride=spread), :] for q in range(2)
            ]
            fsend[h, :, j * LANES:(j + 1) * LANES] = jnp.concatenate(two, axis=0).astype(BF16)

    copies = []
    for k in range(n_dp - 1, 0, -1):
        to = partner(d, k, n_dp)
        copy = pltpu.make_async_remote_copy(
            src_ref=fsend.at[to % 2],
            dst_ref=fall.at[d],
            send_sem=f_send.at[to],
            recv_sem=f_recv.at[d],
            device_id={"dp": to, "mp": m},
            device_id_type=pl.DeviceIdType.MESH,
        )
        copy.start()
        copies.append((to, copy))
    fall[d] = fsend[core]

    load_query.wait()
    their_rows = pl.ds(pl.multiple_of((1 - core) * rows_q, 16), rows_q)
    pltpu.make_async_remote_copy(
        src_ref=query_hbm.at[:, half_of(1 - core)],
        dst_ref=qbuf.at[their_rows],
        send_sem=qx_send,
        recv_sem=qx_recv,
        device_id={"dp": sibling, "mp": m},
        device_id_type=pl.DeviceIdType.MESH,
    ).wait_recv()
    for k in range(1, n_dp):
        source = partner(d, k, n_dp) if n_dp & (n_dp - 1) == 0 else (d + n_dp - k) % n_dp
        pltpu.make_async_remote_copy(
            src_ref=fsend.at[0],
            dst_ref=fall.at[source],
            send_sem=f_send.at[source],
            recv_sem=f_recv.at[source],
            device_id={"dp": source, "mp": m},
            device_id_type=pl.DeviceIdType.MESH,
        ).wait_recv()

    feats = fall[...].reshape(n_dp * 2 * EX_DEV, quarter)
    score = []
    for q in range(2):
        score.append(
            lax.dot_general(
                feats, qbuf[:, q * quarter:(q + 1) * quarter], NT, preferred_element_type=F32
            ).reshape(n_dp, 2, EX_DEV, 2 * rows_q)[:, q]
        )
    scores = (score[0] + score[1]).reshape(n_dp * EX_DEV, 2 * rows_q).T
    part[...] = scores.reshape(groups, rows_out, n_dp * EX_DEV)

    mine = core * n_mp + m
    sent = []
    for k in range(n_mp):
        for s in range(2):
            if k == 0 and s == 0:
                continue
            to_m = partner(m, k, n_mp)
            to_core = flipped(core, s)
            slot = to_core * n_mp + to_m
            copy = pltpu.make_async_remote_copy(
                src_ref=part.at[slot],
                dst_ref=prec.at[mine],
                send_sem=p_send.at[slot],
                recv_sem=p_recv.at[mine],
                device_id={"dp": flipped(d, s), "mp": to_m},
                device_id_type=pl.DeviceIdType.MESH,
            )
            copy.start()
            sent.append(copy)
    total = part[mine]
    for k in range(n_mp):
        for s in range(2):
            if k == 0 and s == 0:
                continue
            from_m = partner(m, k, n_mp) if n_mp & (n_mp - 1) == 0 else (m + n_mp - k) % n_mp
            slot = flipped(core, s) * n_mp + from_m
            pltpu.make_async_remote_copy(
                src_ref=part.at[slot],
                dst_ref=prec.at[slot],
                send_sem=p_send.at[slot],
                recv_sem=p_recv.at[slot],
                device_id={"dp": flipped(d, s), "mp": from_m},
                device_id_type=pl.DeviceIdType.MESH,
            ).wait_recv()
            total = total + prec[slot]
    out_ref[...] = total
    for to, copy in copies:
        copy.wait_send()
    query_copy.wait_send()
    for copy in sent:
        copy.wait_send()


def shards(n_dp, n_mp, token_factors, example_ids, left_factor, right_factor, query_features):
    tokens, rank = token_factors.shape[1], left_factor.shape[1]
    rows_q, feat = query_features.shape
    rows_out = rows_q // n_mp
    groups = 2 * n_mp
    train = n_dp * EX_DEV
    dma = pltpu.SemaphoreType.DMA
    vmem = pl.BlockSpec(memory_space=pltpu.VMEM)
    in_hbm = pl.BlockSpec(memory_space=pltpu.HBM)
    return pl.pallas_call(
        functools.partial(kernel, n_dp, n_mp),
        out_shape=pltpu.VMEM((rows_out, train), F32),
        in_specs=[in_hbm] * 5,
        out_specs=vmem,
        scratch_shapes=[
            pltpu.VMEM((tokens, 2 * rank), BF16),
            pltpu.VMEM((1, tokens), jnp.int32),
            pltpu.VMEM((rank, rank), BF16),
            pltpu.VMEM((rank, rank), BF16),
            pltpu.VMEM((EX_DEV * rank, EX_DEV * rank), BF16),
            pltpu.VMEM((4 * rank, 2 * rank), F32),
            pltpu.VMEM((2 * rows_q, feat // 2), BF16),
            pltpu.VMEM((2, 2 * EX_DEV, feat // 4), BF16),
            pltpu.VMEM((n_dp, 2 * EX_DEV, feat // 4), BF16),
            pltpu.VMEM((groups, rows_out, train), F32),
            pltpu.VMEM((groups, rows_out, train), F32),
            dma((4,)), dma, dma, dma,
            dma((n_dp,)), dma((n_dp,)),
            dma((groups,)), dma((groups,)),
        ],
        compiler_params=pltpu.CompilerParams(
            collective_id=0, has_side_effects=True, vmem_limit_bytes=16 * 1024 * 1024
        ),
        cost_estimate=pl.CostEstimate(
            flops=2 * rank * EX_DEV * tokens * 2 * rank, bytes_accessed=2 * rows_q * feat,
            transcendentals=0,
        ),
    )(*(
        pltpu.with_memory_space_constraint(array, pltpu.HBM)
        for array in (token_factors, example_ids, left_factor, right_factor, query_features)
    ))


def solution(mesh):
    placed = (
        P("mp", "dp", None),
        P("dp", None),
        P("mp", None, None),
        P("mp", None, None),
        P("dp", "mp"),
    )
    return jax.shard_map(
        functools.partial(shards, mesh.shape["dp"], mesh.shape["mp"]),
        mesh=mesh, in_specs=placed, out_specs=P(("dp", "mp"), None), check_vma=False,
    )
```

```python
import functools

import jax
import jax.numpy as jnp
from jax import lax
from jax.experimental import pallas as pl
from jax.experimental.pallas import tpu as pltpu
from jax.sharding import PartitionSpec as P

EX_DEV = 8
LANES = 128
F32, BF16 = jnp.float32, jnp.bfloat16
NT = (((1,), (1,)), ((), ()))


def flipped(index, mask):
    bit = 1
    while bit <= mask:
        if mask & bit:
            index = index + bit - 2 * bit * ((index // bit) % 2)
        bit *= 2
    return index


def partner(index, offset, count):
    if count & (count - 1) == 0:
        return flipped(index, offset)
    return (index + offset) % count


def iota(shape, dim):
    return lax.broadcasted_iota(jnp.int32, shape, dim)


def split(value):
    high = value.astype(BF16)
    return high, (value - high.astype(F32)).astype(BF16)


def kernel(
    n_dp, n_mp,
    tokens_hbm, ids_hbm, left_hbm, right_hbm, query_hbm, out_ref,
    tok, ids_ref, left_ref, right_ref, blocks, pscr, qbuf, fsend, fall, part, prec,
    in_sem, q_sem, qx_send, qx_recv, f_send, f_recv, p_send, p_recv,
):
    d, m = lax.axis_index("dp"), lax.axis_index("mp")
    core = d % 2
    sibling = flipped(d, 1)
    tokens = tok.shape[0]
    rank = left_ref.shape[0]
    rows_q = query_hbm.shape[0]
    half = query_hbm.shape[1] // 2
    quarter = half // 2
    rows_out = rows_q // n_mp
    groups = 2 * n_mp

    loads = []
    for i, (source, target) in enumerate(
        ((tokens_hbm.at[0], tok), (ids_hbm, ids_ref), (left_hbm.at[0], left_ref), (right_hbm.at[0], right_ref))
    ):
        loads.append(pltpu.make_async_copy(source, target, in_sem.at[i]))
        loads[-1].start()

    barrier = pltpu.get_barrier_semaphore()
    for k in range(1, n_dp):
        pl.semaphore_signal(barrier, inc=1, device_id={"dp": partner(d, k, n_dp), "mp": m})
    for k in range(1, n_mp):
        for s in range(2):
            pl.semaphore_signal(
                barrier, inc=1, device_id={"dp": flipped(d, s), "mp": partner(m, k, n_mp)}
            )

    def half_of(which):
        return pl.ds(pl.multiple_of(which * half, LANES), half)

    my_rows = pl.ds(pl.multiple_of(core * rows_q, 16), rows_q)
    load_query = pltpu.make_async_copy(query_hbm.at[:, half_of(core)], qbuf.at[my_rows], q_sem)
    load_query.start()

    for load in loads:
        load.wait()
    tall, wide = 2 * rank, EX_DEV * rank
    ids = ids_ref[...]
    member = (ids == iota((EX_DEV, tokens), 0)).astype(F32)
    inverse = 1.0 / jnp.sum(member, axis=1, keepdims=True)
    group = iota((1, 4 * rank), 1) // rank
    scale = []
    for i in range(2):
        row = jnp.zeros((1, 4 * rank), F32)
        for j in range(4):
            row = jnp.where(group == j, inverse[2 * j + i:2 * j + i + 1, :], row)
        scale.append(jnp.broadcast_to(row, (rank, 4 * rank)))
    scale = jnp.concatenate(scale, axis=0)

    step = 512
    turn = (iota((tall, tall), 1) == iota((tall, tall), 0)).astype(BF16)
    none = jnp.zeros((rank, step), BF16)
    summed = jnp.zeros((tall, 4 * rank), F32)
    for start in range(0, tokens, step):
        turned = lax.dot_general(
            turn, tok[start:start + step, :], NT, preferred_element_type=F32
        ).astype(BF16)
        inputs, outputs = turned[:rank], turned[rank:]
        here = ids[:, start:start + step]
        lhs = jnp.concatenate([jnp.where(here % 2 == i, outputs, none) for i in range(2)], axis=0)
        rhs = jnp.concatenate([jnp.where(here // 2 == j, inputs, none) for j in range(4)], axis=0)
        summed = summed + lax.dot_general(lhs, rhs, NT, preferred_element_type=F32)
    grad = summed * scale

    widen = (iota((rank, tall), 1) % rank == iota((rank, tall), 0)).astype(BF16)
    rows = (
        iota((tall, rank), 1) == 2 * (iota((tall, rank), 0) % (rank // 2)) + iota((tall, rank), 0) // rank
    ).astype(BF16)
    left = jnp.dot(left_ref[...], widen, preferred_element_type=F32).astype(BF16)
    left = jnp.dot(rows, left, preferred_element_type=F32)
    same = iota((tall, tall), 1) // rank == (iota((tall, tall), 0) // (rank // 2)) % 2
    left = jnp.where(same, left, 0.0).astype(BF16)
    left = jnp.concatenate([left, left], axis=1)
    widest = (iota((rank, wide), 1) % rank == iota((rank, wide), 0)).astype(BF16)
    right = jnp.dot(right_ref[...], widest, preferred_element_type=F32)
    column = iota((rank, wide), 1) // rank
    for p in range(2):
        for j in range(4):
            at = (p * 4 + j) * rank
            blocks[at:at + rank, :] = jnp.where(column == 2 * j + p, right, 0.0).astype(BF16)

    high, low = split(grad)
    mixed = jnp.dot(left, jnp.concatenate([high, low], axis=0), preferred_element_type=F32)
    high, low = split(jnp.concatenate([mixed[:rank], mixed[rank:]], axis=1))
    both = jnp.dot(jnp.concatenate([high, low], axis=0), blocks[...], preferred_element_type=F32)
    precond = both[:rank] + both[rank:]
    for j in range(4):
        pscr[j * rank:(j + 1) * rank, :] = precond[:, j * LANES:(j + 1) * LANES]
    spread = rank // 2
    tiles = spread // 4
    for h in range(2):
        for j in range(tiles):
            two = [
                pscr[pl.ds((h * 2 + q) * tiles + j, EX_DEV, stride=spread), :] for q in range(2)
            ]
            fsend[h, :, j * LANES:(j + 1) * LANES] = jnp.concatenate(two, axis=0).astype(BF16)

    pl.semaphore_wait(barrier, n_dp - 1 + 2 * (n_mp - 1))

    copies = []
    for k in range(n_dp - 1, 0, -1):
        to = partner(d, k, n_dp)
        copy = pltpu.make_async_remote_copy(
            src_ref=fsend.at[to % 2],
            dst_ref=fall.at[d],
            send_sem=f_send.at[to],
            recv_sem=f_recv.at[d],
            device_id={"dp": to, "mp": m},
            device_id_type=pl.DeviceIdType.MESH,
        )
        copy.start()
        copies.append((to, copy))
    query_copy = pltpu.make_async_remote_copy(
        src_ref=query_hbm.at[:, half_of(1 - core)],
        dst_ref=qbuf.at[my_rows],
        send_sem=qx_send,
        recv_sem=qx_recv,
        device_id={"dp": sibling, "mp": m},
        device_id_type=pl.DeviceIdType.MESH,
    )
    query_copy.start()
    fall[d] = fsend[core]

    load_query.wait()
    for k in range(1, n_dp):
        source = partner(d, k, n_dp) if n_dp & (n_dp - 1) == 0 else (d + n_dp - k) % n_dp
        pltpu.make_async_remote_copy(
            src_ref=fsend.at[0],
            dst_ref=fall.at[source],
            send_sem=f_send.at[source],
            recv_sem=f_recv.at[source],
            device_id={"dp": source, "mp": m},
            device_id_type=pl.DeviceIdType.MESH,
        ).wait_recv()

    feats = fall[...].reshape(n_dp * 2 * EX_DEV, quarter)
    their_rows = pl.ds(pl.multiple_of((1 - core) * rows_q, 16), rows_q)
    mine = core * n_mp + m
    sent = []
    for s in range(2):
        to_core = flipped(core, s)
        if s == 1:
            pltpu.make_async_remote_copy(
                src_ref=query_hbm.at[:, half_of(1 - core)],
                dst_ref=qbuf.at[their_rows],
                send_sem=qx_send,
                recv_sem=qx_recv,
                device_id={"dp": sibling, "mp": m},
                device_id_type=pl.DeviceIdType.MESH,
            ).wait_recv()
        at = their_rows if s else my_rows
        score = []
        for q in range(2):
            score.append(
                lax.dot_general(
                    feats, qbuf[at, q * quarter:(q + 1) * quarter], NT, preferred_element_type=F32
                ).reshape(n_dp, 2, EX_DEV, rows_q)[:, q]
            )
        scores = (score[0] + score[1]).reshape(n_dp * EX_DEV, rows_q).T
        part[pl.ds(to_core * n_mp, n_mp)] = scores.reshape(n_mp, rows_out, n_dp * EX_DEV)
        for k in range(n_mp - 1, -1, -1):
            if k == 0 and s == 0:
                continue
            to_m = partner(m, k, n_mp)
            slot = to_core * n_mp + to_m
            copy = pltpu.make_async_remote_copy(
                src_ref=part.at[slot],
                dst_ref=prec.at[mine],
                send_sem=p_send.at[slot],
                recv_sem=p_recv.at[mine],
                device_id={"dp": flipped(d, s), "mp": to_m},
                device_id_type=pl.DeviceIdType.MESH,
            )
            copy.start()
            sent.append(copy)
    total = part[mine]
    for k in range(n_mp):
        for s in range(2):
            if k == 0 and s == 0:
                continue
            from_m = partner(m, k, n_mp) if n_mp & (n_mp - 1) == 0 else (m + n_mp - k) % n_mp
            slot = flipped(core, s) * n_mp + from_m
            pltpu.make_async_remote_copy(
                src_ref=part.at[slot],
                dst_ref=prec.at[slot],
                send_sem=p_send.at[slot],
                recv_sem=p_recv.at[slot],
                device_id={"dp": flipped(d, s), "mp": from_m},
                device_id_type=pl.DeviceIdType.MESH,
            ).wait_recv()
            total = total + prec[slot]
    out_ref[...] = total
    for to, copy in copies:
        copy.wait_send()
    query_copy.wait_send()
    for copy in sent:
        copy.wait_send()


def shards(n_dp, n_mp, token_factors, example_ids, left_factor, right_factor, query_features):
    tokens, rank = token_factors.shape[1], left_factor.shape[1]
    rows_q, feat = query_features.shape
    rows_out = rows_q // n_mp
    groups = 2 * n_mp
    train = n_dp * EX_DEV
    dma = pltpu.SemaphoreType.DMA
    vmem = pl.BlockSpec(memory_space=pltpu.VMEM)
    in_hbm = pl.BlockSpec(memory_space=pltpu.HBM)
    return pl.pallas_call(
        functools.partial(kernel, n_dp, n_mp),
        out_shape=pltpu.VMEM((rows_out, train), F32),
        in_specs=[in_hbm] * 5,
        out_specs=vmem,
        scratch_shapes=[
            pltpu.VMEM((tokens, 2 * rank), BF16),
            pltpu.VMEM((1, tokens), jnp.int32),
            pltpu.VMEM((rank, rank), BF16),
            pltpu.VMEM((rank, rank), BF16),
            pltpu.VMEM((EX_DEV * rank, EX_DEV * rank), BF16),
            pltpu.VMEM((4 * rank, 2 * rank), F32),
            pltpu.VMEM((2 * rows_q, feat // 2), BF16),
            pltpu.VMEM((2, 2 * EX_DEV, feat // 4), BF16),
            pltpu.VMEM((n_dp, 2 * EX_DEV, feat // 4), BF16),
            pltpu.VMEM((groups, rows_out, train), F32),
            pltpu.VMEM((groups, rows_out, train), F32),
            dma((4,)), dma, dma, dma,
            dma((n_dp,)), dma((n_dp,)),
            dma((groups,)), dma((groups,)),
        ],
        compiler_params=pltpu.CompilerParams(
            collective_id=0, has_side_effects=True, vmem_limit_bytes=16 * 1024 * 1024
        ),
        cost_estimate=pl.CostEstimate(
            flops=2 * rank * EX_DEV * tokens * 2 * rank, bytes_accessed=2 * rows_q * feat,
            transcendentals=0,
        ),
    )(*(
        pltpu.with_memory_space_constraint(array, pltpu.HBM)
        for array in (token_factors, example_ids, left_factor, right_factor, query_features)
    ))


def solution(mesh):
    placed = (
        P("mp", "dp", None),
        P("dp", None),
        P("mp", None, None),
        P("mp", None, None),
        P("dp", "mp"),
    )
    return jax.shard_map(
        functools.partial(shards, mesh.shape["dp"], mesh.shape["mp"]),
        mesh=mesh, in_specs=placed, out_specs=P(("dp", "mp"), None), check_vma=False,
    )
```

```python
import functools

import jax
import jax.numpy as jnp
from jax import lax
from jax.experimental import pallas as pl
from jax.experimental.pallas import tpu as pltpu
from jax.sharding import PartitionSpec as P

EX_DEV = 8
LANES = 128
F32, BF16 = jnp.float32, jnp.bfloat16
NT = (((1,), (1,)), ((), ()))


def flipped(index, mask):
    bit = 1
    while bit <= mask:
        if mask & bit:
            index = index + bit - 2 * bit * ((index // bit) % 2)
        bit *= 2
    return index


def partner(index, offset, count):
    if count & (count - 1) == 0:
        return flipped(index, offset)
    return (index + offset) % count


def iota(shape, dim):
    return lax.broadcasted_iota(jnp.int32, shape, dim)


def split(value):
    high = value.astype(BF16)
    return high, (value - high.astype(F32)).astype(BF16)


def kernel(
    n_dp, n_mp,
    tokens_hbm, ids_hbm, left_hbm, right_hbm, query_hbm, out_ref,
    tok, ids_ref, left_ref, right_ref, blocks, pscr, qbuf, fsend, fall, part, prec,
    in_sem, q_sem, qx_send, qx_recv, f_send, f_recv, p_send, p_recv,
):
    d, m = lax.axis_index("dp"), lax.axis_index("mp")
    core = d % 2
    sibling = flipped(d, 1)
    tokens = tok.shape[0]
    rank = left_ref.shape[0]
    rows_q = query_hbm.shape[0]
    half = query_hbm.shape[1] // 2
    quarter = half // 2
    rows_out = rows_q // n_mp
    groups = 2 * n_mp

    loads = []
    for i, (source, target) in enumerate(
        ((ids_hbm, ids_ref), (left_hbm.at[0], left_ref), (right_hbm.at[0], right_ref), (tokens_hbm.at[0], tok))
    ):
        loads.append(pltpu.make_async_copy(source, target, in_sem.at[i]))
        loads[-1].start()

    barrier = pltpu.get_barrier_semaphore()
    for k in range(1, n_dp):
        pl.semaphore_signal(barrier, inc=1, device_id={"dp": partner(d, k, n_dp), "mp": m})
    for k in range(1, n_mp):
        for s in range(2):
            pl.semaphore_signal(
                barrier, inc=1, device_id={"dp": flipped(d, s), "mp": partner(m, k, n_mp)}
            )

    def half_of(which):
        return pl.ds(pl.multiple_of(which * half, LANES), half)

    my_rows = pl.ds(pl.multiple_of(core * rows_q, 16), rows_q)
    load_query = pltpu.make_async_copy(query_hbm.at[:, half_of(core)], qbuf.at[my_rows], q_sem)
    load_query.start()

    for load in loads[:3]:
        load.wait()
    tall, wide = 2 * rank, EX_DEV * rank
    ids = ids_ref[...]
    member = (ids == iota((EX_DEV, tokens), 0)).astype(F32)
    inverse = 1.0 / jnp.sum(member, axis=1, keepdims=True)
    group = iota((1, 4 * rank), 1) // rank
    scale = []
    for i in range(2):
        row = jnp.zeros((1, 4 * rank), F32)
        for j in range(4):
            row = jnp.where(group == j, inverse[2 * j + i:2 * j + i + 1, :], row)
        scale.append(jnp.broadcast_to(row, (rank, 4 * rank)))
    scale = jnp.concatenate(scale, axis=0)

    widen = (iota((rank, tall), 1) % rank == iota((rank, tall), 0)).astype(BF16)
    rows = (
        iota((tall, rank), 1) == 2 * (iota((tall, rank), 0) % (rank // 2)) + iota((tall, rank), 0) // rank
    ).astype(BF16)
    left = jnp.dot(left_ref[...], widen, preferred_element_type=F32).astype(BF16)
    left = jnp.dot(rows, left, preferred_element_type=F32)
    same = iota((tall, tall), 1) // rank == (iota((tall, tall), 0) // (rank // 2)) % 2
    left = jnp.where(same, left, 0.0).astype(BF16)
    left = jnp.concatenate([left, left], axis=1)
    widest = (iota((rank, wide), 1) % rank == iota((rank, wide), 0)).astype(BF16)
    right = jnp.dot(right_ref[...], widest, preferred_element_type=F32)
    column = iota((rank, wide), 1) // rank
    for p in range(2):
        for j in range(4):
            at = (p * 4 + j) * rank
            blocks[at:at + rank, :] = jnp.where(column == 2 * j + p, right, 0.0).astype(BF16)

    loads[3].wait()
    step = 512
    turn = (iota((tall, tall), 1) == iota((tall, tall), 0)).astype(BF16)
    none = jnp.zeros((rank, step), BF16)
    summed = jnp.zeros((tall, 4 * rank), F32)
    for start in range(0, tokens, step):
        turned = lax.dot_general(
            turn, tok[start:start + step, :], NT, preferred_element_type=F32
        ).astype(BF16)
        inputs, outputs = turned[:rank], turned[rank:]
        here = ids[:, start:start + step]
        lhs = jnp.concatenate([jnp.where(here % 2 == i, outputs, none) for i in range(2)], axis=0)
        rhs = jnp.concatenate([jnp.where(here // 2 == j, inputs, none) for j in range(4)], axis=0)
        summed = summed + lax.dot_general(lhs, rhs, NT, preferred_element_type=F32)
    grad = summed * scale

    high, low = split(grad)
    mixed = jnp.dot(left, jnp.concatenate([high, low], axis=0), preferred_element_type=F32)
    high, low = split(jnp.concatenate([mixed[:rank], mixed[rank:]], axis=1))
    both = jnp.dot(jnp.concatenate([high, low], axis=0), blocks[...], preferred_element_type=F32)
    precond = both[:rank] + both[rank:]
    for j in range(4):
        pscr[j * rank:(j + 1) * rank, :] = precond[:, j * LANES:(j + 1) * LANES]
    spread = rank // 2
    tiles = spread // 4
    for h in range(2):
        for j in range(tiles):
            two = [
                pscr[pl.ds((h * 2 + q) * tiles + j, EX_DEV, stride=spread), :] for q in range(2)
            ]
            fsend[h, :, j * LANES:(j + 1) * LANES] = jnp.concatenate(two, axis=0).astype(BF16)

    pl.semaphore_wait(barrier, n_dp - 1 + 2 * (n_mp - 1))

    copies = []
    for k in range(n_dp - 1, 0, -1):
        to = partner(d, k, n_dp)
        copy = pltpu.make_async_remote_copy(
            src_ref=fsend.at[to % 2],
            dst_ref=fall.at[d],
            send_sem=f_send.at[to],
            recv_sem=f_recv.at[d],
            device_id={"dp": to, "mp": m},
            device_id_type=pl.DeviceIdType.MESH,
        )
        copy.start()
        copies.append((to, copy))
    query_copy = pltpu.make_async_remote_copy(
        src_ref=query_hbm.at[:, half_of(1 - core)],
        dst_ref=qbuf.at[my_rows],
        send_sem=qx_send,
        recv_sem=qx_recv,
        device_id={"dp": sibling, "mp": m},
        device_id_type=pl.DeviceIdType.MESH,
    )
    query_copy.start()
    fall[d] = fsend[core]

    load_query.wait()
    for k in range(1, n_dp):
        source = partner(d, k, n_dp) if n_dp & (n_dp - 1) == 0 else (d + n_dp - k) % n_dp
        pltpu.make_async_remote_copy(
            src_ref=fsend.at[0],
            dst_ref=fall.at[source],
            send_sem=f_send.at[source],
            recv_sem=f_recv.at[source],
            device_id={"dp": source, "mp": m},
            device_id_type=pl.DeviceIdType.MESH,
        ).wait_recv()

    feats = fall[...].reshape(n_dp * 2 * EX_DEV, quarter)
    their_rows = pl.ds(pl.multiple_of((1 - core) * rows_q, 16), rows_q)
    mine = core * n_mp + m
    sent = []
    for s in range(2):
        to_core = flipped(core, s)
        if s == 1:
            pltpu.make_async_remote_copy(
                src_ref=query_hbm.at[:, half_of(1 - core)],
                dst_ref=qbuf.at[their_rows],
                send_sem=qx_send,
                recv_sem=qx_recv,
                device_id={"dp": sibling, "mp": m},
                device_id_type=pl.DeviceIdType.MESH,
            ).wait_recv()
        at = their_rows if s else my_rows
        score = []
        for q in range(2):
            score.append(
                lax.dot_general(
                    feats, qbuf[at, q * quarter:(q + 1) * quarter], NT, preferred_element_type=F32
                ).reshape(n_dp, 2, EX_DEV, rows_q)[:, q]
            )
        scores = (score[0] + score[1]).reshape(n_dp * EX_DEV, rows_q).T
        part[pl.ds(to_core * n_mp, n_mp)] = scores.reshape(n_mp, rows_out, n_dp * EX_DEV)
        for k in range(n_mp - 1, -1, -1):
            if k == 0 and s == 0:
                continue
            to_m = partner(m, k, n_mp)
            slot = to_core * n_mp + to_m
            copy = pltpu.make_async_remote_copy(
                src_ref=part.at[slot],
                dst_ref=prec.at[mine],
                send_sem=p_send.at[slot],
                recv_sem=p_recv.at[mine],
                device_id={"dp": flipped(d, s), "mp": to_m},
                device_id_type=pl.DeviceIdType.MESH,
            )
            copy.start()
            sent.append(copy)
    total = part[mine]
    for k in range(n_mp):
        for s in range(2):
            if k == 0 and s == 0:
                continue
            from_m = partner(m, k, n_mp) if n_mp & (n_mp - 1) == 0 else (m + n_mp - k) % n_mp
            slot = flipped(core, s) * n_mp + from_m
            pltpu.make_async_remote_copy(
                src_ref=part.at[slot],
                dst_ref=prec.at[slot],
                send_sem=p_send.at[slot],
                recv_sem=p_recv.at[slot],
                device_id={"dp": flipped(d, s), "mp": from_m},
                device_id_type=pl.DeviceIdType.MESH,
            ).wait_recv()
            total = total + prec[slot]
    out_ref[...] = total
    for to, copy in copies:
        copy.wait_send()
    query_copy.wait_send()
    for copy in sent:
        copy.wait_send()


def shards(n_dp, n_mp, token_factors, example_ids, left_factor, right_factor, query_features):
    tokens, rank = token_factors.shape[1], left_factor.shape[1]
    rows_q, feat = query_features.shape
    rows_out = rows_q // n_mp
    groups = 2 * n_mp
    train = n_dp * EX_DEV
    dma = pltpu.SemaphoreType.DMA
    vmem = pl.BlockSpec(memory_space=pltpu.VMEM)
    in_hbm = pl.BlockSpec(memory_space=pltpu.HBM)
    return pl.pallas_call(
        functools.partial(kernel, n_dp, n_mp),
        out_shape=pltpu.VMEM((rows_out, train), F32),
        in_specs=[in_hbm] * 5,
        out_specs=vmem,
        scratch_shapes=[
            pltpu.VMEM((tokens, 2 * rank), BF16),
            pltpu.VMEM((1, tokens), jnp.int32),
            pltpu.VMEM((rank, rank), BF16),
            pltpu.VMEM((rank, rank), BF16),
            pltpu.VMEM((EX_DEV * rank, EX_DEV * rank), BF16),
            pltpu.VMEM((4 * rank, 2 * rank), F32),
            pltpu.VMEM((2 * rows_q, feat // 2), BF16),
            pltpu.VMEM((2, 2 * EX_DEV, feat // 4), BF16),
            pltpu.VMEM((n_dp, 2 * EX_DEV, feat // 4), BF16),
            pltpu.VMEM((groups, rows_out, train), F32),
            pltpu.VMEM((groups, rows_out, train), F32),
            dma((4,)), dma, dma, dma,
            dma((n_dp,)), dma((n_dp,)),
            dma((groups,)), dma((groups,)),
        ],
        compiler_params=pltpu.CompilerParams(
            collective_id=0, has_side_effects=True, vmem_limit_bytes=16 * 1024 * 1024
        ),
        cost_estimate=pl.CostEstimate(
            flops=2 * rank * EX_DEV * tokens * 2 * rank, bytes_accessed=2 * rows_q * feat,
            transcendentals=0,
        ),
    )(*(
        pltpu.with_memory_space_constraint(array, pltpu.HBM)
        for array in (token_factors, example_ids, left_factor, right_factor, query_features)
    ))


def solution(mesh):
    placed = (
        P("mp", "dp", None),
        P("dp", None),
        P("mp", None, None),
        P("mp", None, None),
        P("dp", "mp"),
    )
    return jax.shard_map(
        functools.partial(shards, mesh.shape["dp"], mesh.shape["mp"]),
        mesh=mesh, in_specs=placed, out_specs=P(("dp", "mp"), None), check_vma=False,
    )
```

```python
import functools

import jax
import jax.numpy as jnp
from jax import lax
from jax.experimental import pallas as pl
from jax.experimental.pallas import tpu as pltpu
from jax.sharding import PartitionSpec as P

EX_DEV = 8
LANES = 128
F32, BF16 = jnp.float32, jnp.bfloat16
NT = (((1,), (1,)), ((), ()))


def flipped(index, mask):
    bit = 1
    while bit <= mask:
        if mask & bit:
            index = index + bit - 2 * bit * ((index // bit) % 2)
        bit *= 2
    return index


def partner(index, offset, count):
    if count & (count - 1) == 0:
        return flipped(index, offset)
    return (index + offset) % count


def iota(shape, dim):
    return lax.broadcasted_iota(jnp.int32, shape, dim)


def split(value):
    high = value.astype(BF16)
    return high, (value - high.astype(F32)).astype(BF16)


def kernel(
    n_dp, n_mp,
    tokens_hbm, ids_hbm, left_hbm, right_hbm, query_hbm, out_ref,
    tok, ids_ref, left_ref, right_ref, blocks, pscr, qbuf, fsend, fall, part, prec,
    in_sem, q_sem, qx_send, qx_recv, f_send, f_recv, p_send, p_recv,
):
    d, m = lax.axis_index("dp"), lax.axis_index("mp")
    core = d % 2
    sibling = flipped(d, 1)
    tokens = tok.shape[0]
    rank = left_ref.shape[0]
    rows_q = query_hbm.shape[0]
    half = query_hbm.shape[1] // 2
    quarter = half // 2
    rows_out = rows_q // n_mp
    groups = 2 * n_mp

    loads = []
    for i, (source, target) in enumerate(
        ((tokens_hbm.at[0], tok), (ids_hbm, ids_ref), (left_hbm.at[0], left_ref), (right_hbm.at[0], right_ref))
    ):
        loads.append(pltpu.make_async_copy(source, target, in_sem.at[i]))
        loads[-1].start()

    barrier = pltpu.get_barrier_semaphore()
    for k in range(1, n_dp):
        pl.semaphore_signal(barrier, inc=1, device_id={"dp": partner(d, k, n_dp), "mp": m})
    for k in range(1, n_mp):
        for s in range(2):
            pl.semaphore_signal(
                barrier, inc=1, device_id={"dp": flipped(d, s), "mp": partner(m, k, n_mp)}
            )

    def half_of(which):
        return pl.ds(pl.multiple_of(which * half, LANES), half)

    my_rows = pl.ds(pl.multiple_of(core * rows_q, 16), rows_q)
    load_query = pltpu.make_async_copy(query_hbm.at[:, half_of(core)], qbuf.at[my_rows], q_sem)
    load_query.start()

    for load in loads:
        load.wait()
    tall, wide = 2 * rank, EX_DEV * rank
    ids = ids_ref[...]
    member = (ids == iota((EX_DEV, tokens), 0)).astype(F32)
    inverse = 1.0 / jnp.sum(member, axis=1, keepdims=True)
    group = iota((1, 4 * rank), 1) // rank
    scale = []
    for i in range(2):
        row = jnp.zeros((1, 4 * rank), F32)
        for j in range(4):
            row = jnp.where(group == j, inverse[2 * j + i:2 * j + i + 1, :], row)
        scale.append(jnp.broadcast_to(row, (rank, 4 * rank)))
    scale = jnp.concatenate(scale, axis=0)

    step = 512
    turn = (iota((tall, tall), 1) == iota((tall, tall), 0)).astype(BF16)
    none = jnp.zeros((rank, step), BF16)
    summed = jnp.zeros((tall, 4 * rank), F32)
    for start in range(0, tokens, step):
        turned = lax.dot_general(
            turn, tok[start:start + step, :], NT, preferred_element_type=F32
        ).astype(BF16)
        inputs, outputs = turned[:rank], turned[rank:]
        here = ids[:, start:start + step]
        lhs = jnp.concatenate([jnp.where(here % 2 == i, outputs, none) for i in range(2)], axis=0)
        rhs = jnp.concatenate([jnp.where(here // 2 == j, inputs, none) for j in range(4)], axis=0)
        summed = summed + lax.dot_general(lhs, rhs, NT, preferred_element_type=F32)
    grad = summed * scale

    widen = (iota((rank, tall), 1) % rank == iota((rank, tall), 0)).astype(BF16)
    rows = (
        iota((tall, rank), 1) == 2 * (iota((tall, rank), 0) % (rank // 2)) + iota((tall, rank), 0) // rank
    ).astype(BF16)
    left = jnp.dot(left_ref[...], widen, preferred_element_type=F32).astype(BF16)
    left = jnp.dot(rows, left, preferred_element_type=F32)
    same = iota((tall, tall), 1) // rank == (iota((tall, tall), 0) // (rank // 2)) % 2
    left = jnp.where(same, left, 0.0).astype(BF16)
    left = jnp.concatenate([left, left], axis=1)
    widest = (iota((rank, wide), 1) % rank == iota((rank, wide), 0)).astype(BF16)
    right = jnp.dot(right_ref[...], widest, preferred_element_type=F32)
    column = iota((rank, wide), 1) // rank
    for p in range(2):
        for j in range(4):
            at = (p * 4 + j) * rank
            blocks[at:at + rank, :] = jnp.where(column == 2 * j + p, right, 0.0).astype(BF16)

    high, low = split(grad)
    mixed = jnp.dot(left, jnp.concatenate([high, low], axis=0), preferred_element_type=F32)
    high, low = split(jnp.concatenate([mixed[:rank], mixed[rank:]], axis=1))
    both = jnp.dot(jnp.concatenate([high, low], axis=0), blocks[...], preferred_element_type=F32)
    precond = both[:rank] + both[rank:]
    for j in range(4):
        pscr[j * rank:(j + 1) * rank, :] = precond[:, j * LANES:(j + 1) * LANES]
    spread = rank // 2
    tiles = spread // 4
    pl.semaphore_wait(barrier, n_dp - 1 + 2 * (n_mp - 1))

    copies = []

    def send_features(to):
        copy = pltpu.make_async_remote_copy(
            src_ref=fsend.at[to % 2],
            dst_ref=fall.at[d],
            send_sem=f_send.at[to],
            recv_sem=f_recv.at[d],
            device_id={"dp": to, "mp": m},
            device_id_type=pl.DeviceIdType.MESH,
        )
        copy.start()
        copies.append((to, copy))

    for h in range(2):
        for j in range(tiles):
            two = [
                pscr[pl.ds((h * 2 + q) * tiles + j, EX_DEV, stride=spread), :] for q in range(2)
            ]
            fsend[h, :, j * LANES:(j + 1) * LANES] = jnp.concatenate(two, axis=0).astype(BF16)
        for k in range(n_dp // 2 - 1, 0, -1):
            send_features(2 * partner(d // 2, k, n_dp // 2) + h)

    send_features(sibling)
    query_copy = pltpu.make_async_remote_copy(
        src_ref=query_hbm.at[:, half_of(1 - core)],
        dst_ref=qbuf.at[my_rows],
        send_sem=qx_send,
        recv_sem=qx_recv,
        device_id={"dp": sibling, "mp": m},
        device_id_type=pl.DeviceIdType.MESH,
    )
    query_copy.start()
    fall[d] = fsend[core]

    load_query.wait()
    for k in range(1, n_dp):
        source = partner(d, k, n_dp) if n_dp & (n_dp - 1) == 0 else (d + n_dp - k) % n_dp
        pltpu.make_async_remote_copy(
            src_ref=fsend.at[0],
            dst_ref=fall.at[source],
            send_sem=f_send.at[source],
            recv_sem=f_recv.at[source],
            device_id={"dp": source, "mp": m},
            device_id_type=pl.DeviceIdType.MESH,
        ).wait_recv()

    feats = fall[...].reshape(n_dp * 2 * EX_DEV, quarter)
    their_rows = pl.ds(pl.multiple_of((1 - core) * rows_q, 16), rows_q)
    mine = core * n_mp + m
    sent = []
    for s in range(2):
        to_core = flipped(core, s)
        if s == 1:
            pltpu.make_async_remote_copy(
                src_ref=query_hbm.at[:, half_of(1 - core)],
                dst_ref=qbuf.at[their_rows],
                send_sem=qx_send,
                recv_sem=qx_recv,
                device_id={"dp": sibling, "mp": m},
                device_id_type=pl.DeviceIdType.MESH,
            ).wait_recv()
        at = their_rows if s else my_rows
        score = []
        for q in range(2):
            score.append(
                lax.dot_general(
                    feats, qbuf[at, q * quarter:(q + 1) * quarter], NT, preferred_element_type=F32
                ).reshape(n_dp, 2, EX_DEV, rows_q)[:, q]
            )
        scores = (score[0] + score[1]).reshape(n_dp * EX_DEV, rows_q).T
        part[pl.ds(to_core * n_mp, n_mp)] = scores.reshape(n_mp, rows_out, n_dp * EX_DEV)
        for k in range(n_mp - 1, -1, -1):
            if k == 0 and s == 0:
                continue
            to_m = partner(m, k, n_mp)
            slot = to_core * n_mp + to_m
            copy = pltpu.make_async_remote_copy(
                src_ref=part.at[slot],
                dst_ref=prec.at[mine],
                send_sem=p_send.at[slot],
                recv_sem=p_recv.at[mine],
                device_id={"dp": flipped(d, s), "mp": to_m},
                device_id_type=pl.DeviceIdType.MESH,
            )
            copy.start()
            sent.append(copy)
    total = part[mine]
    for k in range(n_mp):
        for s in range(2):
            if k == 0 and s == 0:
                continue
            from_m = partner(m, k, n_mp) if n_mp & (n_mp - 1) == 0 else (m + n_mp - k) % n_mp
            slot = flipped(core, s) * n_mp + from_m
            pltpu.make_async_remote_copy(
                src_ref=part.at[slot],
                dst_ref=prec.at[slot],
                send_sem=p_send.at[slot],
                recv_sem=p_recv.at[slot],
                device_id={"dp": flipped(d, s), "mp": from_m},
                device_id_type=pl.DeviceIdType.MESH,
            ).wait_recv()
            total = total + prec[slot]
    out_ref[...] = total
    for to, copy in copies:
        copy.wait_send()
    query_copy.wait_send()
    for copy in sent:
        copy.wait_send()


def shards(n_dp, n_mp, token_factors, example_ids, left_factor, right_factor, query_features):
    tokens, rank = token_factors.shape[1], left_factor.shape[1]
    rows_q, feat = query_features.shape
    rows_out = rows_q // n_mp
    groups = 2 * n_mp
    train = n_dp * EX_DEV
    dma = pltpu.SemaphoreType.DMA
    vmem = pl.BlockSpec(memory_space=pltpu.VMEM)
    in_hbm = pl.BlockSpec(memory_space=pltpu.HBM)
    return pl.pallas_call(
        functools.partial(kernel, n_dp, n_mp),
        out_shape=pltpu.VMEM((rows_out, train), F32),
        in_specs=[in_hbm] * 5,
        out_specs=vmem,
        scratch_shapes=[
            pltpu.VMEM((tokens, 2 * rank), BF16),
            pltpu.VMEM((1, tokens), jnp.int32),
            pltpu.VMEM((rank, rank), BF16),
            pltpu.VMEM((rank, rank), BF16),
            pltpu.VMEM((EX_DEV * rank, EX_DEV * rank), BF16),
            pltpu.VMEM((4 * rank, 2 * rank), F32),
            pltpu.VMEM((2 * rows_q, feat // 2), BF16),
            pltpu.VMEM((2, 2 * EX_DEV, feat // 4), BF16),
            pltpu.VMEM((n_dp, 2 * EX_DEV, feat // 4), BF16),
            pltpu.VMEM((groups, rows_out, train), F32),
            pltpu.VMEM((groups, rows_out, train), F32),
            dma((4,)), dma, dma, dma,
            dma((n_dp,)), dma((n_dp,)),
            dma((groups,)), dma((groups,)),
        ],
        compiler_params=pltpu.CompilerParams(
            collective_id=0, has_side_effects=True, vmem_limit_bytes=16 * 1024 * 1024
        ),
        cost_estimate=pl.CostEstimate(
            flops=2 * rank * EX_DEV * tokens * 2 * rank, bytes_accessed=2 * rows_q * feat,
            transcendentals=0,
        ),
    )(*(
        pltpu.with_memory_space_constraint(array, pltpu.HBM)
        for array in (token_factors, example_ids, left_factor, right_factor, query_features)
    ))


def solution(mesh):
    placed = (
        P("mp", "dp", None),
        P("dp", None),
        P("mp", None, None),
        P("mp", None, None),
        P("dp", "mp"),
    )
    return jax.shard_map(
        functools.partial(shards, mesh.shape["dp"], mesh.shape["mp"]),
        mesh=mesh, in_specs=placed, out_specs=P(("dp", "mp"), None), check_vma=False,
    )
```
